32 devices in a mesh: groups: 2 (over y), tmpl: 4 (over z), chan: 2 (over x), tm: 2 (over core).
Axes of the slice: x: 2, y: 2, z: 4, core: 2. Of those that a mesh axis runs over, the one named last changes fastest.
Arguments:
- samples: bfloat16 [1792, 3584], P(('tmpl', 'chan'), ('groups', 'tm')), parts along dimension 1, may hold values from -6 to 6
- tail: bfloat16 [1792, 1792], P(('tmpl', 'chan'), 'groups'), parts along dimension 1, may hold values from -6 to 6
- templates: bfloat16 [128, 8, 640], P('tmpl', 'chan'), may hold values from -6 to 6
- channels: int32 [128, 8], P('tmpl', 'chan'), may hold values from 0 to 1791
- moveouts: int32 [128, 8], P('tmpl', 'chan'), may hold values from 0 to 256
- live: int32 [128], P('tmpl'), may hold values from 4 to 8
Outputs:
- detection: float32 [128, 3584], P(('tmpl', 'chan'), ('groups', 'tm')), parts along dimension 1
The draws below stay inside these ranges and needn't reach their ends.
There are 2 independent parts, one for each index of `groups`. The reference program is written for one: setup_inputs(seed, part) draws one part's arguments, and reference() takes and returns one part's arrays. A program takes and returns all parts, laid end to end along the dimension named above; an argument that names none is the same for every part. Nothing has to cross between parts.
All inputs are finite; a program needn't handle non-finite values.
Results may differ from the reference program's by a relative error of at most 0.0003.
Values may be sent and summed in bfloat16 or wider, within the bound.
A program may use at most 64 MiB of HBM per device.

```python
import jax
import jax.numpy as jnp
from jax import lax

CH = 1792
L = 640
MAXS = 256
K = 8
NT = 128
TIME = 1792
HALO = 896


def place_ends(drawn, key, low, top_value):
    index_at = [jax.random.randint(jax.random.fold_in(key, axis), (), 0, length) for axis, length in enumerate(drawn.shape)]
    widest = drawn.shape.index(max(drawn.shape))
    next_to = index_at[:widest] + [(index_at[widest] + 1) % drawn.shape[widest]] + index_at[widest + 1:]
    return drawn.at[tuple(index_at)].set(low).at[tuple(next_to)].set(top_value)


def block_levels(stream_key, extent, shards, low, largest):
    loudness, own = 1.0, jax.random.fold_in(stream_key, 6)
    for axis_at, parts in shards:
        heights = jnp.exp(jax.random.uniform(jax.random.fold_in(own, axis_at), (parts,), jnp.float32, low / len(shards), largest / len(shards)))
        loudness = loudness * jnp.repeat(heights, extent[axis_at] // parts).reshape([-1 if axis == axis_at else 1 for axis in range(len(extent))])
    return loudness


def centred(rng, extent, deviation, limit, shards=(), kind=jnp.bfloat16):
    entries = jax.random.normal(rng, extent, jnp.float32) * deviation
    if len(shards) > 0:
        entries = block_levels(rng, extent, shards, -0.22, 0.18) * entries
    return jnp.clip(entries, min=-limit, max=limit).astype(kind)


def setup_inputs(seed: int = 0, part: int = 0) -> dict:
    splits = jax.random.split(jax.random.key(seed), 7)
    part_splits = jax.random.split(jax.random.fold_in(splits[6], part), 7)
    samples = centred(part_splits[0], (CH, TIME), 1.0, 6.0, ((0, 8), (1, 2)))
    tail = centred(part_splits[1], (CH, HALO), 1.0, 6.0, ((0, 8),))
    templates = centred(splits[2], (NT, K, L), 1.0, 6.0, ((0, 4), (1, 2)))
    channels = place_ends(jax.random.randint(splits[3], (NT, K), 0, CH), jax.random.fold_in(splits[3], 1), 0, CH - 1).astype(jnp.int32)
    moveouts = place_ends(jax.random.randint(splits[4], (NT, K), 0, MAXS + 1), jax.random.fold_in(splits[4], 1), 0, MAXS).astype(jnp.int32)
    live = place_ends(jax.random.randint(splits[5], (NT,), K // 2, K + 1), jax.random.fold_in(splits[5], 1), K // 2, K).astype(jnp.int32)
    return {"samples": samples, "tail": tail, "templates": templates, "channels": channels, "moveouts": moveouts, "live": live}


EPS = 1e-06

def depthwise(signal, kernel, precision):
    output = lax.conv_general_dilated(signal[None], kernel[:, None, :], (1,), 'VALID', dimension_numbers=('NCH', 'OIH', 'NCH'), feature_group_count=signal.shape[0], precision=precision, preferred_element_type=jnp.float32)
    return output[0]

def shifted_rows(window, chan_ids, offsets, length):
    picked = jnp.take(window, chan_ids, axis=0)

    def one_row(row_data, offset):
        return lax.dynamic_slice_in_dim(row_data, offset.astype(jnp.int32), length)
    return jax.vmap(one_row)(picked, offsets)

def reference(samples, tail, templates, channels, moveouts, live):
    window = jnp.concatenate([samples, tail], axis=1)

    def one_template(packed):
        waveform, chan_ids, offsets, used = packed
        slot_data = shifted_rows(window, chan_ids, offsets, TIME + L)
        correlation = depthwise(slot_data, waveform, None)[:, :TIME]
        squares = slot_data.astype(jnp.float32) ** 2
        energy = depthwise(squares, jnp.ones((K, L), jnp.float32), lax.Precision.HIGHEST)[:, :TIME]
        tnorm = jnp.sqrt(lax.optimization_barrier(jnp.sum(waveform.astype(jnp.float32) ** 2, axis=-1)) + EPS)
        ncc = correlation / (tnorm[:, None] * jnp.sqrt(energy + EPS))
        used_f = used.astype(jnp.float32)
        weight = jnp.where(jnp.arange(K) < used, jnp.sqrt(jnp.float32(L) / used_f), jnp.float32(0.0))
        return lax.optimization_barrier(jnp.sum(weight[:, None] * ncc, axis=0))
    return lax.map(one_template, (templates, channels, moveouts, live))
```

```python
import functools

import jax
import jax.numpy as jnp
from jax import lax
from jax.experimental import pallas as pl
from jax.experimental.pallas import tpu as pltpu
from jax.sharding import PartitionSpec as P

EPS = 1e-06
LANES = 128
GROUP = 8
STEP = 32
PIECES = LANES // STEP
VMEM_LIMIT = 60 * 1024 * 1024


def rolled(value, distance):
    size = value.shape[1]
    return pltpu.roll(value, (size - distance) % size, 1)


def window_kernel(length, samples_ref, rim_ref, wide_ref, scale_ref):
    block, rim = samples_ref.shape[1], rim_ref.shape[1]
    extent, starts = wide_ref.shape[1], scale_ref.shape[1]
    rows = 16

    @pl.loop(0, samples_ref.shape[0] // rows)
    def _(i):
        at = pl.ds(pl.multiple_of(i * rows, rows), rows)
        pieces = [samples_ref[at, :].astype(jnp.float32), rim_ref[at, :].astype(jnp.float32)]
        if extent > block + rim:
            pieces.append(jnp.zeros((rows, extent - block - rim), jnp.float32))
        wide = jnp.concatenate(pieces, axis=1)
        wide_ref[at, :] = wide
        total = wide * wide
        reach = 1
        while reach < LANES:
            total = total + rolled(total, reach)
            reach *= 2
        energy = total[:, :starts]
        for c in range(1, length // LANES):
            energy = energy + total[:, c * LANES : c * LANES + starts]
        scale_ref[at, :] = lax.rsqrt(energy + EPS)


def detect_kernel(
    groups_ref, slot_ref, row_ref, chan_ref, move_ref, weight_ref,
    waves_ref, wide_ref, scale_ref, out_ref,
    waves, picked, lined, shifts, spread, own, found,
):
    block = out_ref.shape[1]
    length = waves_ref.shape[1]
    count = length // STEP
    span = shifts.shape[1]
    taken = span + LANES
    scaled = block + LANES
    out_ref[...] = jnp.zeros_like(out_ref)

    @pl.loop(0, waves_ref.shape[0] // LANES)
    def _(i):
        at = pl.ds(pl.multiple_of(i * LANES, LANES), LANES)
        waves[at, :] = waves_ref[at, :].astype(jnp.float32)

    width = GROUP * STEP
    k_id = lax.broadcasted_iota(jnp.int32, (LANES, width), 0)
    r_id = lax.broadcasted_iota(jnp.int32, (LANES, width), 1) // GROUP
    for q in range(PIECES):
        spread[:, q * width : (q + 1) * width] = (k_id == r_id + q * STEP).astype(jnp.float32).astype(jnp.bfloat16)
    row_id = lax.broadcasted_iota(jnp.int32, (count // PIECES * GROUP, width), 0) % GROUP
    col_id = lax.broadcasted_iota(jnp.int32, (count // PIECES * GROUP, width), 1) % GROUP
    own[...] = (row_id == col_id).astype(jnp.float32)

    @pl.loop(0, groups_ref[0])
    def _(g):
        for i in range(GROUP):
            s = g * GROUP + i
            move = move_ref[s]
            coarse = pl.multiple_of((move // LANES) * LANES, LANES)
            fine = move % LANES
            picked[i : i + 1, :] = waves[pl.ds(slot_ref[s], 1), :]
            row = wide_ref[pl.ds(chan_ref[s], 1), pl.ds(coarse, taken)]
            lined[i : i + 1, :] = pltpu.roll(row, taken - fine, 1)
        wave = picked[...]
        tnorm = lax.rsqrt(jnp.sum(wave * wave, axis=1, keepdims=True) + EPS)
        for r in range(0, STEP, 2):
            pair = [rolled(lined[...], r + k)[:, :span] if r + k else lined[:, :span] for k in range(2)]
            shifts[r * GROUP : (r + 2) * GROUP, :] = jnp.concatenate(pair, axis=0).astype(jnp.bfloat16)
        blocks = count // PIECES
        stacked = jnp.concatenate([wave[:, j * LANES : (j + 1) * LANES] for j in range(blocks)], axis=0)
        expanded = jnp.dot(stacked.astype(jnp.bfloat16), spread[...], preferred_element_type=jnp.float32)
        mask = own[...]
        left = jnp.concatenate([expanded[:, q * width : (q + 1) * width] * mask for q in range(PIECES)], axis=0)
        product = jnp.dot(left.astype(jnp.bfloat16), shifts[...], preferred_element_type=jnp.float32)
        total = None
        for q in range(PIECES):
            part = None
            for j in range(blocks):
                at = (q * blocks + j) * GROUP
                term = product[at : at + GROUP, j * LANES : j * LANES + scaled]
                part = term if part is None else part + term
            if q:
                part = rolled(part, q * STEP)
            total = part if total is None else total + part
        found[...] = total[:, :block] * tnorm
        for i in range(GROUP):
            s = g * GROUP + i
            move = move_ref[s]
            coarse = pl.multiple_of((move // LANES) * LANES, LANES)
            fine = move % LANES
            scale = scale_ref[pl.ds(chan_ref[s], 1), pl.ds(coarse, scaled)]
            scale = pltpu.roll(scale, scaled - fine, 1)[:, :block]
            at = pl.ds(row_ref[s], 1)
            out_ref[at, :] += found[i : i + 1, :] * scale * weight_ref[s]


def vmem():
    return pl.BlockSpec(memory_space=pltpu.VMEM)


def smem():
    return pl.BlockSpec(memory_space=pltpu.SMEM)


def up(value, multiple):
    return -(-value // multiple) * multiple


def body(samples, tail, templates, channels, moveouts, live):
    chans, block = samples.shape
    per_dev, per_slot, length = templates.shape
    slots = per_dev * per_slot
    axes = ("tmpl", "chan")
    n_chan = lax.axis_size("chan")
    parts = lax.axis_size("tmpl") * n_chan
    me = lax.axis_index("tmpl") * n_chan + lax.axis_index("chan")
    n_rows = per_dev * lax.axis_size("tmpl")
    max_live, max_move = 64, 512

    slot_index = lax.axis_index("chan") * per_slot + jnp.arange(per_slot)
    code = (channels * max_move + moveouts) * max_live + live[:, None]
    code = jnp.where(slot_index[None, :] < live[:, None], code, -1).reshape(slots)
    codes = lax.all_gather(code, axes, axis=0, tiled=True)
    waveform = templates.reshape(slots, length)
    waves = lax.all_gather(waveform, axes, axis=0, tiled=True)

    devices = lax.axis_size("tm")
    route = [(i, i - 1) for i in range(1, devices)]
    following = lax.ppermute(samples, "tm", route)
    rim = jnp.where(lax.axis_index("tm") == devices - 1, tail[:, :block], following)

    padded = up(chans, 16)
    if padded != chans:
        samples = jnp.pad(samples, ((0, padded - chans), (0, 0)))
        rim = jnp.pad(rim, ((0, padded - chans), (0, 0)))
    starts = block + 3 * LANES
    extent = max(starts + length, block + rim.shape[1])
    wide, scale = pl.pallas_call(
        functools.partial(window_kernel, length),
        out_shape=(
            jax.ShapeDtypeStruct((padded, extent), jnp.float32),
            jax.ShapeDtypeStruct((padded, starts), jnp.float32),
        ),
        in_specs=[vmem(), vmem()],
        out_specs=(vmem(), vmem()),
        compiler_params=pltpu.CompilerParams(vmem_limit_bytes=VMEM_LIMIT),
    )(samples, rim)

    total = parts * slots
    index = jnp.arange(total)
    chan = codes // (max_move * max_live)
    mine = (codes >= 0) & (chan // chans == me)
    before = jnp.sum((index[None, :] < index[:, None]) & mine[None, :], axis=1, dtype=jnp.int32)
    number = jnp.sum(mine, dtype=jnp.int32)
    hit = (before[None, :] == index[:, None]) & mine[None, :]
    slot = jnp.sum(jnp.where(hit, index[None, :], 0), axis=1, dtype=jnp.int32)
    picked_code = jnp.sum(jnp.where(hit, codes[None, :], 0), axis=1, dtype=jnp.int32)
    used = index < number
    owner = slot // slots
    row = (owner // n_chan) * per_dev + (slot % slots) // per_slot
    local = jnp.where(used, picked_code // (max_move * max_live) - me * chans, 0)
    move = (picked_code // max_live) % max_move
    live_f = jnp.maximum(picked_code % max_live, 1).astype(jnp.float32)
    weight = jnp.where(used, jnp.sqrt(jnp.float32(length) / live_f), 0.0)
    groups = ((number + GROUP - 1) // GROUP).reshape(1)

    span = up(block + length - STEP, LANES)
    partial_value = pl.pallas_call(
        detect_kernel,
        out_shape=jax.ShapeDtypeStruct((n_rows, block), jnp.float32),
        in_specs=[smem()] * 6 + [vmem()] * 3,
        out_specs=vmem(),
        scratch_shapes=[
            pltpu.VMEM((total, length), jnp.float32),
            pltpu.VMEM((GROUP, length), jnp.float32),
            pltpu.VMEM((GROUP, span + LANES), jnp.float32),
            pltpu.VMEM((GROUP * STEP, span), jnp.bfloat16),
            pltpu.VMEM((LANES, PIECES * GROUP * STEP), jnp.bfloat16),
            pltpu.VMEM((length // LANES * GROUP, GROUP * STEP), jnp.float32),
            pltpu.VMEM((GROUP, block), jnp.float32),
        ],
        compiler_params=pltpu.CompilerParams(vmem_limit_bytes=VMEM_LIMIT),
    )(groups, slot, row, local, move, weight, waves, wide, scale)
    return lax.psum_scatter(partial_value, axes, scatter_dimension=0, tiled=True)


def solution(mesh):
    in_specs = (
        P(("tmpl", "chan"), ("groups", "tm")),
        P(("tmpl", "chan"), "groups"),
        P("tmpl", "chan", None),
        P("tmpl", "chan"),
        P("tmpl", "chan"),
        P("tmpl"),
    )
    out_specs = P(("tmpl", "chan"), ("groups", "tm"))
    return jax.shard_map(body, mesh=mesh, in_specs=in_specs, out_specs=out_specs, check_vma=False)
```

```python
import functools

import jax
import jax.numpy as jnp
from jax import lax
from jax.experimental import pallas as pl
from jax.experimental.pallas import tpu as pltpu
from jax.sharding import PartitionSpec as P

EPS = 1e-06
LANES = 128
GROUP = 8
STEP = 32
PIECES = LANES // STEP
VMEM_LIMIT = 60 * 1024 * 1024


def rolled(value, distance):
    size = value.shape[1]
    return pltpu.roll(value, (size - distance) % size, 1)


def window_kernel(length, samples_ref, rim_ref, wide_ref, scale_ref):
    block, rim = samples_ref.shape[1], rim_ref.shape[1]
    extent, starts = wide_ref.shape[1], scale_ref.shape[1]
    rows = 16

    @pl.loop(0, samples_ref.shape[0] // rows)
    def _(i):
        at = pl.ds(pl.multiple_of(i * rows, rows), rows)
        pieces = [samples_ref[at, :].astype(jnp.float32), rim_ref[at, :].astype(jnp.float32)]
        if extent > block + rim:
            pieces.append(jnp.zeros((rows, extent - block - rim), jnp.float32))
        wide = jnp.concatenate(pieces, axis=1)
        wide_ref[at, :] = wide
        total = wide * wide
        reach = 1
        while reach < LANES:
            total = total + rolled(total, reach)
            reach *= 2
        energy = total[:, :starts]
        for c in range(1, length // LANES):
            energy = energy + total[:, c * LANES : c * LANES + starts]
        scale_ref[at, :] = lax.rsqrt(energy + EPS)


def detect_kernel(
    groups_ref, slot_ref, row_ref, chan_ref, move_ref, weight_ref,
    waves_ref, wide_ref, scale_ref, out_ref,
    waves, picked, lined, shifts, spread, own, found,
):
    block = out_ref.shape[1]
    length = waves_ref.shape[1]
    count = length // STEP
    span = shifts.shape[1]
    taken = span + LANES
    scaled = block + LANES
    out_ref[...] = jnp.zeros_like(out_ref)

    @pl.loop(0, waves_ref.shape[0] // LANES)
    def _(i):
        at = pl.ds(pl.multiple_of(i * LANES, LANES), LANES)
        waves[at, :] = waves_ref[at, :].astype(jnp.float32)

    width = GROUP * STEP
    k_id = lax.broadcasted_iota(jnp.int32, (LANES, width), 0)
    r_id = lax.broadcasted_iota(jnp.int32, (LANES, width), 1) // GROUP
    for q in range(PIECES):
        spread[:, q * width : (q + 1) * width] = (k_id == r_id + q * STEP).astype(jnp.float32).astype(jnp.bfloat16)
    row_id = lax.broadcasted_iota(jnp.int32, (count // PIECES * GROUP, width), 0) % GROUP
    col_id = lax.broadcasted_iota(jnp.int32, (count // PIECES * GROUP, width), 1) % GROUP
    own[...] = (row_id == col_id).astype(jnp.float32)

    @pl.loop(0, groups_ref[0])
    def _(g):
        for i in range(GROUP):
            s = g * GROUP + i
            move = move_ref[s]
            coarse = pl.multiple_of((move // LANES) * LANES, LANES)
            fine = move % LANES
            picked[i : i + 1, :] = waves[pl.ds(slot_ref[s], 1), :]
            row = wide_ref[pl.ds(chan_ref[s], 1), pl.ds(coarse, taken)]
            lined[i : i + 1, :] = pltpu.roll(row, taken - fine, 1)
        wave = picked[...]
        tnorm = lax.rsqrt(jnp.sum(wave * wave, axis=1, keepdims=True) + EPS)
        for r in range(0, STEP, 2):
            pair = [rolled(lined[...], r + k)[:, :span] if r + k else lined[:, :span] for k in range(2)]
            shifts[r * GROUP : (r + 2) * GROUP, :] = jnp.concatenate(pair, axis=0).astype(jnp.bfloat16)
        blocks = count // PIECES
        stacked = jnp.concatenate([wave[:, j * LANES : (j + 1) * LANES] for j in range(blocks)], axis=0)
        expanded = jnp.dot(stacked.astype(jnp.bfloat16), spread[...], preferred_element_type=jnp.float32)
        mask = own[...]
        left = jnp.concatenate([expanded[:, q * width : (q + 1) * width] * mask for q in range(PIECES)], axis=0)
        product = jnp.dot(left.astype(jnp.bfloat16), shifts[...], preferred_element_type=jnp.float32)
        total = None
        for q in range(PIECES):
            part = None
            for j in range(blocks):
                at = (q * blocks + j) * GROUP
                term = product[at : at + GROUP, j * LANES : j * LANES + scaled]
                part = term if part is None else part + term
            if q:
                part = rolled(part, q * STEP)
            total = part if total is None else total + part
        found[...] = total[:, :block] * tnorm
        for i in range(GROUP):
            s = g * GROUP + i
            move = move_ref[s]
            coarse = pl.multiple_of((move // LANES) * LANES, LANES)
            fine = move % LANES
            scale = scale_ref[pl.ds(chan_ref[s], 1), pl.ds(coarse, scaled)]
            scale = pltpu.roll(scale, scaled - fine, 1)[:, :block]
            at = pl.ds(row_ref[s], 1)
            out_ref[at, :] += found[i : i + 1, :] * scale * weight_ref[s]


def greet(peers):
    barrier = pltpu.get_barrier_semaphore()
    for peer in peers:
        pl.semaphore_signal(barrier, inc=1, device_id=peer, device_id_type=pl.DeviceIdType.MESH)
    pl.semaphore_wait(barrier, len(peers))


def scatter_kernel(value_ref, out_ref, across, sums, along, x_send, x_recv, z_send, z_recv):
    n_z, n_x = lax.axis_size("tmpl"), lax.axis_size("chan")
    z, x = lax.axis_index("tmpl"), lax.axis_index("chan")
    x_peers = [{"chan": lax.rem(x + j, n_x)} for j in range(1, n_x)]
    z_peers = [{"tmpl": lax.rem(z + k, n_z)} for k in range(1, n_z)]
    greet(x_peers + z_peers)
    order = [*range(1, n_z), 0]
    copies = {}
    for k in order:
        for j in range(1, n_x):
            there = lax.rem(z + k, n_z) * n_x + lax.rem(x + j, n_x)
            copies["x", k, j] = pltpu.make_async_remote_copy(
                value_ref.at[there], across.at[k, j - 1], x_send.at[k, j - 1], x_recv.at[k, j - 1],
                device_id=x_peers[j - 1], device_id_type=pl.DeviceIdType.MESH,
            )
            copies["x", k, j].start()
    for k in order:
        total = value_ref[lax.rem(z + k, n_z) * n_x + x]
        for j in range(1, n_x):
            copies["x", k, j].wait_recv()
            total = total + across[k, j - 1]
        sums[k] = total
        if k:
            copies["z", k] = pltpu.make_async_remote_copy(
                sums.at[k], along.at[k - 1], z_send.at[k - 1], z_recv.at[k - 1],
                device_id=z_peers[k - 1], device_id_type=pl.DeviceIdType.MESH,
            )
            copies["z", k].start()
    total = sums[0]
    for k in range(1, n_z):
        copies["z", k].wait_recv()
        total = total + along[k - 1]
    out_ref[...] = total
    for copy in copies.values():
        copy.wait_send()


def scattered(value):
    n_z, n_x = lax.axis_size("tmpl"), lax.axis_size("chan")
    keep, block = value.shape[0] // (n_z * n_x), value.shape[1]
    return pl.pallas_call(
        scatter_kernel,
        out_shape=jax.ShapeDtypeStruct((keep, block), jnp.float32),
        in_specs=[vmem()],
        out_specs=vmem(),
        scratch_shapes=[
            pltpu.VMEM((n_z, n_x - 1, keep, block), jnp.float32),
            pltpu.VMEM((n_z, keep, block), jnp.float32),
            pltpu.VMEM((n_z - 1, keep, block), jnp.float32),
            pltpu.SemaphoreType.DMA((n_z, n_x - 1)),
            pltpu.SemaphoreType.DMA((n_z, n_x - 1)),
            pltpu.SemaphoreType.DMA((n_z - 1,)),
            pltpu.SemaphoreType.DMA((n_z - 1,)),
        ],
        compiler_params=pltpu.CompilerParams(
            collective_id=1, has_side_effects=True, vmem_limit_bytes=VMEM_LIMIT
        ),
    )(value.reshape(n_z * n_x, keep, block))


def vmem():
    return pl.BlockSpec(memory_space=pltpu.VMEM)


def smem():
    return pl.BlockSpec(memory_space=pltpu.SMEM)


def up(value, multiple):
    return -(-value // multiple) * multiple


def body(samples, tail, templates, channels, moveouts, live):
    chans, block = samples.shape
    per_dev, per_slot, length = templates.shape
    slots = per_dev * per_slot
    axes = ("tmpl", "chan")
    n_chan = lax.axis_size("chan")
    parts = lax.axis_size("tmpl") * n_chan
    me = lax.axis_index("tmpl") * n_chan + lax.axis_index("chan")
    n_rows = per_dev * lax.axis_size("tmpl")
    max_live, max_move = 64, 512

    slot_index = lax.axis_index("chan") * per_slot + jnp.arange(per_slot)
    code = (channels * max_move + moveouts) * max_live + live[:, None]
    code = jnp.where(slot_index[None, :] < live[:, None], code, -1).reshape(slots)
    codes = lax.all_gather(code, axes, axis=0, tiled=True)
    waveform = templates.reshape(slots, length)
    waves = lax.all_gather(waveform, axes, axis=0, tiled=True)

    devices = lax.axis_size("tm")
    route = [(i, i - 1) for i in range(1, devices)]
    following = lax.ppermute(samples, "tm", route)
    rim = jnp.where(lax.axis_index("tm") == devices - 1, tail[:, :block], following)

    padded = up(chans, 16)
    if padded != chans:
        samples = jnp.pad(samples, ((0, padded - chans), (0, 0)))
        rim = jnp.pad(rim, ((0, padded - chans), (0, 0)))
    starts = block + 3 * LANES
    extent = max(starts + length, block + rim.shape[1])
    wide, scale = pl.pallas_call(
        functools.partial(window_kernel, length),
        out_shape=(
            jax.ShapeDtypeStruct((padded, extent), jnp.float32),
            jax.ShapeDtypeStruct((padded, starts), jnp.float32),
        ),
        in_specs=[vmem(), vmem()],
        out_specs=(vmem(), vmem()),
        compiler_params=pltpu.CompilerParams(vmem_limit_bytes=VMEM_LIMIT),
    )(samples, rim)

    total = parts * slots
    index = jnp.arange(total)
    chan = codes // (max_move * max_live)
    mine = (codes >= 0) & (chan // chans == me)
    before = jnp.sum((index[None, :] < index[:, None]) & mine[None, :], axis=1, dtype=jnp.int32)
    number = jnp.sum(mine, dtype=jnp.int32)
    hit = (before[None, :] == index[:, None]) & mine[None, :]
    slot = jnp.sum(jnp.where(hit, index[None, :], 0), axis=1, dtype=jnp.int32)
    picked_code = jnp.sum(jnp.where(hit, codes[None, :], 0), axis=1, dtype=jnp.int32)
    used = index < number
    owner = slot // slots
    row = (owner // n_chan) * per_dev + (slot % slots) // per_slot
    local = jnp.where(used, picked_code // (max_move * max_live) - me * chans, 0)
    move = (picked_code // max_live) % max_move
    live_f = jnp.maximum(picked_code % max_live, 1).astype(jnp.float32)
    weight = jnp.where(used, jnp.sqrt(jnp.float32(length) / live_f), 0.0)
    groups = ((number + GROUP - 1) // GROUP).reshape(1)

    span = up(block + length - STEP, LANES)
    partial_value = pl.pallas_call(
        detect_kernel,
        out_shape=jax.ShapeDtypeStruct((n_rows, block), jnp.float32),
        in_specs=[smem()] * 6 + [vmem()] * 3,
        out_specs=vmem(),
        scratch_shapes=[
            pltpu.VMEM((total, length), jnp.float32),
            pltpu.VMEM((GROUP, length), jnp.float32),
            pltpu.VMEM((GROUP, span + LANES), jnp.float32),
            pltpu.VMEM((GROUP * STEP, span), jnp.bfloat16),
            pltpu.VMEM((LANES, PIECES * GROUP * STEP), jnp.bfloat16),
            pltpu.VMEM((length // LANES * GROUP, GROUP * STEP), jnp.float32),
            pltpu.VMEM((GROUP, block), jnp.float32),
        ],
        compiler_params=pltpu.CompilerParams(vmem_limit_bytes=VMEM_LIMIT),
    )(groups, slot, row, local, move, weight, waves, wide, scale)
    return scattered(partial_value)


def solution(mesh):
    in_specs = (
        P(("tmpl", "chan"), ("groups", "tm")),
        P(("tmpl", "chan"), "groups"),
        P("tmpl", "chan", None),
        P("tmpl", "chan"),
        P("tmpl", "chan"),
        P("tmpl"),
    )
    out_specs = P(("tmpl", "chan"), ("groups", "tm"))
    return jax.shard_map(body, mesh=mesh, in_specs=in_specs, out_specs=out_specs, check_vma=False)
```

```python
import functools

import jax
import jax.numpy as jnp
from jax import lax
from jax.experimental import pallas as pl
from jax.experimental.pallas import tpu as pltpu
from jax.sharding import PartitionSpec as P

EPS = 1e-06
LANES = 128
GROUP = 8
ROWS = 16
STEP = 32
PIECES = LANES // STEP
VMEM_LIMIT = 60 * 1024 * 1024


def rolled(value, distance):
    size = value.shape[1]
    return pltpu.roll(value, (size - distance) % size, 1)


def window_rows(length, samples_ref, halo, tail_ref, is_last, wide_ref, scale_ref, first, last):
    block, rim = samples_ref.shape[1], tail_ref.shape[1]
    extent, starts = wide_ref.shape[1], scale_ref.shape[1]
    if first == last:
        return

    @pl.loop(first, last)
    def _(i):
        at = pl.ds(pl.multiple_of(i * ROWS, ROWS), ROWS)
        after = jnp.where(is_last, tail_ref[at, :].astype(jnp.float32), halo[at, :].astype(jnp.float32))
        pieces = [samples_ref[at, :].astype(jnp.float32), after]
        if extent > block + rim:
            pieces.append(jnp.zeros((ROWS, extent - block - rim), jnp.float32))
        wide = jnp.concatenate(pieces, axis=1)
        wide_ref[at, :] = wide
        total = wide * wide
        reach = 1
        while reach < LANES:
            total = total + rolled(total, reach)
            reach *= 2
        energy = total[:, :starts]
        for c in range(1, length // LANES):
            energy = energy + total[:, c * LANES : c * LANES + starts]
        scale_ref[at, :] = lax.rsqrt(energy + EPS)


def gather_kernel(
    length, own_ref, code_ref, samples_ref, tail_ref,
    waves_ref, codes_ref, wide_ref, scale_ref,
    halo, halo_sems, code_send, code_recv, z_send, z_recv, x_send, x_recv, c_send, c_recv,
):
    n_z, n_x, n_c = (lax.axis_size(a) for a in ("tmpl", "chan", "tm"))
    z, x, c = (lax.axis_index(a) for a in ("tmpl", "chan", "tm"))
    me = z * n_x + x
    share = own_ref.shape[0] // n_c
    rows = pl.ds(pl.multiple_of(c * share, share), share)
    far = [(k, j) for k in range(n_z) for j in range(n_x) if k or j]

    def ahead(k, j):
        return {"tmpl": lax.rem(z + k, n_z), "chan": lax.rem(x + j, n_x)}

    def sibling(t):
        return {"tm": lax.rem(c + t, n_c)}

    greet([ahead(k, j) for k, j in far] + [sibling(t) for t in range(1, n_c)])
    copies = {}

    def send(name, source, target, send_sem, recv_sem, device):
        copies[name] = pltpu.make_async_remote_copy(
            source, target, send_sem, recv_sem, device_id=device, device_id_type=pl.DeviceIdType.MESH
        )
        copies[name].start()

    def pass_x(k, source, target):
        for j in range(1, n_x):
            send(("x", k, j), source, target, x_send.at[k, j - 1], x_recv.at[k, j - 1], ahead(0, j))

    def pass_core(k, j):
        at = lax.rem(z - k + n_z, n_z) * n_x + lax.rem(x - j + n_x, n_x)
        block = waves_ref.at[at, rows]
        for t in range(1, n_c):
            send(
                ("c", k, j, t), block, block, c_send.at[k * n_x + j, t - 1], c_recv.at[k * n_x + j, t - 1], sibling(t)
            )

    send("halo", samples_ref, halo, halo_sems.at[0], halo_sems.at[1], sibling(n_c - 1))
    for k in range(1, n_z):
        send(("z", k), own_ref.at[rows], waves_ref.at[me, rows], z_send.at[k - 1], z_recv.at[k - 1], ahead(k, 0))
    pass_x(0, own_ref.at[rows], waves_ref.at[me, rows])
    for k, j in far:
        at = k * n_x + j
        send(("code", k, j), code_ref, codes_ref.at[me], code_send.at[at], code_recv.at[at], ahead(k, j))
    waves_ref[me] = own_ref[...]
    codes_ref[me] = code_ref[...]
    copies["halo"].wait_recv()

    steps = samples_ref.shape[0] // ROWS
    marks = [steps * i // (n_z + 1) for i in range(n_z + 2)]
    window = functools.partial(
        window_rows, length, samples_ref, halo, tail_ref, c == n_c - 1, wide_ref, scale_ref
    )
    for k in range(1, n_z):
        window(marks[k - 1], marks[k])
        copies["z", k].wait_recv()
        block = waves_ref.at[lax.rem(z - k + n_z, n_z) * n_x + x, rows]
        pass_x(k, block, block)
        pass_core(k, 0)
    window(marks[n_z - 1], marks[n_z])
    for k in range(n_z):
        for j in range(1, n_x):
            copies["x", k, j].wait_recv()
            pass_core(k, j)
    window(marks[n_z], marks[n_z + 1])
    for k, j in far:
        copies["code", k, j].wait_recv()
        for t in range(1, n_c):
            copies["c", k, j, t].wait_recv()
    for copy in copies.values():
        copy.wait_send()


def detect_kernel(
    groups_ref, slot_ref, row_ref, chan_ref, move_ref, weight_ref,
    waves_ref, wide_ref, scale_ref, out_ref,
    waves, picked, lined, shifts, spread, own, found,
):
    block = out_ref.shape[1]
    length = waves_ref.shape[1]
    count = length // STEP
    span = shifts.shape[1]
    taken = span + LANES
    scaled = block + LANES
    out_ref[...] = jnp.zeros_like(out_ref)

    @pl.loop(0, waves_ref.shape[0] // LANES)
    def _(i):
        at = pl.ds(pl.multiple_of(i * LANES, LANES), LANES)
        waves[at, :] = waves_ref[at, :].astype(jnp.float32)

    width = GROUP * STEP
    k_id = lax.broadcasted_iota(jnp.int32, (LANES, width), 0)
    r_id = lax.broadcasted_iota(jnp.int32, (LANES, width), 1) // GROUP
    for q in range(PIECES):
        spread[:, q * width : (q + 1) * width] = (k_id == r_id + q * STEP).astype(jnp.float32).astype(jnp.bfloat16)
    row_id = lax.broadcasted_iota(jnp.int32, (count // PIECES * GROUP, width), 0) % GROUP
    col_id = lax.broadcasted_iota(jnp.int32, (count // PIECES * GROUP, width), 1) % GROUP
    own[...] = (row_id == col_id).astype(jnp.float32)

    @pl.loop(0, groups_ref[0])
    def _(g):
        for i in range(GROUP):
            s = g * GROUP + i
            move = move_ref[s]
            coarse = pl.multiple_of((move // LANES) * LANES, LANES)
            fine = move % LANES
            picked[i : i + 1, :] = waves[pl.ds(slot_ref[s], 1), :]
            row = wide_ref[pl.ds(chan_ref[s], 1), pl.ds(coarse, taken)]
            lined[i : i + 1, :] = pltpu.roll(row, taken - fine, 1)
        wave = picked[...]
        tnorm = lax.rsqrt(jnp.sum(wave * wave, axis=1, keepdims=True) + EPS)
        for r in range(0, STEP, 2):
            pair = [rolled(lined[...], r + k)[:, :span] if r + k else lined[:, :span] for k in range(2)]
            shifts[r * GROUP : (r + 2) * GROUP, :] = jnp.concatenate(pair, axis=0).astype(jnp.bfloat16)
        blocks = count // PIECES
        stacked = jnp.concatenate([wave[:, j * LANES : (j + 1) * LANES] for j in range(blocks)], axis=0)
        expanded = jnp.dot(stacked.astype(jnp.bfloat16), spread[...], preferred_element_type=jnp.float32)
        mask = own[...]
        left = jnp.concatenate([expanded[:, q * width : (q + 1) * width] * mask for q in range(PIECES)], axis=0)
        product = jnp.dot(left.astype(jnp.bfloat16), shifts[...], preferred_element_type=jnp.float32)
        total = None
        for q in range(PIECES):
            part = None
            for j in range(blocks):
                at = (q * blocks + j) * GROUP
                term = product[at : at + GROUP, j * LANES : j * LANES + scaled]
                part = term if part is None else part + term
            if q:
                part = rolled(part, q * STEP)
            total = part if total is None else total + part
        found[...] = total[:, :block] * tnorm
        for i in range(GROUP):
            s = g * GROUP + i
            move = move_ref[s]
            coarse = pl.multiple_of((move // LANES) * LANES, LANES)
            fine = move % LANES
            scale = scale_ref[pl.ds(chan_ref[s], 1), pl.ds(coarse, scaled)]
            scale = pltpu.roll(scale, scaled - fine, 1)[:, :block]
            at = pl.ds(row_ref[s], 1)
            out_ref[at, :] += found[i : i + 1, :] * scale * weight_ref[s]


def greet(peers):
    barrier = pltpu.get_barrier_semaphore()
    for peer in peers:
        pl.semaphore_signal(barrier, inc=1, device_id=peer, device_id_type=pl.DeviceIdType.MESH)
    pl.semaphore_wait(barrier, len(peers))


def scatter_kernel(value_ref, out_ref, across, sums, along, x_send, x_recv, z_send, z_recv):
    n_z, n_x = lax.axis_size("tmpl"), lax.axis_size("chan")
    z, x = lax.axis_index("tmpl"), lax.axis_index("chan")
    x_peers = [{"chan": lax.rem(x + j, n_x)} for j in range(1, n_x)]
    z_peers = [{"tmpl": lax.rem(z + k, n_z)} for k in range(1, n_z)]
    greet(x_peers + z_peers)
    order = [*range(1, n_z), 0]
    copies = {}
    for k in order:
        for j in range(1, n_x):
            there = lax.rem(z + k, n_z) * n_x + lax.rem(x + j, n_x)
            copies["x", k, j] = pltpu.make_async_remote_copy(
                value_ref.at[there], across.at[k, j - 1], x_send.at[k, j - 1], x_recv.at[k, j - 1],
                device_id=x_peers[j - 1], device_id_type=pl.DeviceIdType.MESH,
            )
            copies["x", k, j].start()
    for k in order:
        total = value_ref[lax.rem(z + k, n_z) * n_x + x]
        for j in range(1, n_x):
            copies["x", k, j].wait_recv()
            total = total + across[k, j - 1]
        sums[k] = total
        if k:
            copies["z", k] = pltpu.make_async_remote_copy(
                sums.at[k], along.at[k - 1], z_send.at[k - 1], z_recv.at[k - 1],
                device_id=z_peers[k - 1], device_id_type=pl.DeviceIdType.MESH,
            )
            copies["z", k].start()
    total = sums[0]
    for k in range(1, n_z):
        copies["z", k].wait_recv()
        total = total + along[k - 1]
    out_ref[...] = total
    for copy in copies.values():
        copy.wait_send()


def scattered(value):
    n_z, n_x = lax.axis_size("tmpl"), lax.axis_size("chan")
    keep, block = value.shape[0] // (n_z * n_x), value.shape[1]
    return pl.pallas_call(
        scatter_kernel,
        out_shape=jax.ShapeDtypeStruct((keep, block), jnp.float32),
        in_specs=[vmem()],
        out_specs=vmem(),
        scratch_shapes=[
            pltpu.VMEM((n_z, n_x - 1, keep, block), jnp.float32),
            pltpu.VMEM((n_z, keep, block), jnp.float32),
            pltpu.VMEM((n_z - 1, keep, block), jnp.float32),
            pltpu.SemaphoreType.DMA((n_z, n_x - 1)),
            pltpu.SemaphoreType.DMA((n_z, n_x - 1)),
            pltpu.SemaphoreType.DMA((n_z - 1,)),
            pltpu.SemaphoreType.DMA((n_z - 1,)),
        ],
        compiler_params=pltpu.CompilerParams(
            collective_id=1, has_side_effects=True, vmem_limit_bytes=VMEM_LIMIT
        ),
    )(value.reshape(n_z * n_x, keep, block))


def vmem():
    return pl.BlockSpec(memory_space=pltpu.VMEM)


def smem():
    return pl.BlockSpec(memory_space=pltpu.SMEM)


def up(value, multiple):
    return -(-value // multiple) * multiple


def body(samples, tail, templates, channels, moveouts, live):
    chans, block = samples.shape
    per_dev, per_slot, length = templates.shape
    slots = per_dev * per_slot
    n_chan = lax.axis_size("chan")
    parts = lax.axis_size("tmpl") * n_chan
    me = lax.axis_index("tmpl") * n_chan + lax.axis_index("chan")
    n_rows = per_dev * lax.axis_size("tmpl")
    max_live, max_move = 64, 512

    slot_index = lax.axis_index("chan") * per_slot + jnp.arange(per_slot)
    code = (channels * max_move + moveouts) * max_live + live[:, None]
    code = jnp.where(slot_index[None, :] < live[:, None], code, -1).reshape(slots)
    waveform = templates.reshape(slots, length)
    padded = up(chans, ROWS)
    if padded != chans:
        samples = jnp.pad(samples, ((0, padded - chans), (0, 0)))
        tail = jnp.pad(tail, ((0, padded - chans), (0, 0)))
    starts = block + 3 * LANES
    extent = max(starts + length, block + tail.shape[1])
    n_z, n_c = lax.axis_size("tmpl"), lax.axis_size("tm")

    def sems(*extent):
        return [pltpu.SemaphoreType.DMA(extent)] * 2

    waves, codes, wide, scale = pl.pallas_call(
        functools.partial(gather_kernel, length),
        out_shape=(
            jax.ShapeDtypeStruct((parts, slots, length), jnp.bfloat16),
            jax.ShapeDtypeStruct((parts, 1, slots), jnp.int32),
            jax.ShapeDtypeStruct((padded, extent), jnp.float32),
            jax.ShapeDtypeStruct((padded, starts), jnp.float32),
        ),
        in_specs=[vmem()] * 4,
        out_specs=(vmem(),) * 4,
        scratch_shapes=[
            pltpu.VMEM((padded, block), jnp.bfloat16),
            pltpu.SemaphoreType.DMA((2,)),
            *sems(parts),
            *sems(n_z - 1),
            *sems(n_z, n_chan - 1),
            *sems(parts, n_c - 1),
        ],
        compiler_params=pltpu.CompilerParams(
            collective_id=2, has_side_effects=True, vmem_limit_bytes=VMEM_LIMIT
        ),
    )(waveform, code.reshape(1, slots), samples, tail)
    waves = waves.reshape(parts * slots, length)
    codes = codes.reshape(parts * slots)

    total = parts * slots
    index = jnp.arange(total)
    chan = codes // (max_move * max_live)
    mine = (codes >= 0) & (chan // chans == me)
    before = jnp.sum((index[None, :] < index[:, None]) & mine[None, :], axis=1, dtype=jnp.int32)
    number = jnp.sum(mine, dtype=jnp.int32)
    hit = (before[None, :] == index[:, None]) & mine[None, :]
    slot = jnp.sum(jnp.where(hit, index[None, :], 0), axis=1, dtype=jnp.int32)
    picked_code = jnp.sum(jnp.where(hit, codes[None, :], 0), axis=1, dtype=jnp.int32)
    used = index < number
    owner = slot // slots
    row = (owner // n_chan) * per_dev + (slot % slots) // per_slot
    local = jnp.where(used, picked_code // (max_move * max_live) - me * chans, 0)
    move = (picked_code // max_live) % max_move
    live_f = jnp.maximum(picked_code % max_live, 1).astype(jnp.float32)
    weight = jnp.where(used, jnp.sqrt(jnp.float32(length) / live_f), 0.0)
    groups = ((number + GROUP - 1) // GROUP).reshape(1)

    span = up(block + length - STEP, LANES)
    partial_value = pl.pallas_call(
        detect_kernel,
        out_shape=jax.ShapeDtypeStruct((n_rows, block), jnp.float32),
        in_specs=[smem()] * 6 + [vmem()] * 3,
        out_specs=vmem(),
        scratch_shapes=[
            pltpu.VMEM((total, length), jnp.float32),
            pltpu.VMEM((GROUP, length), jnp.float32),
            pltpu.VMEM((GROUP, span + LANES), jnp.float32),
            pltpu.VMEM((GROUP * STEP, span), jnp.bfloat16),
            pltpu.VMEM((LANES, PIECES * GROUP * STEP), jnp.bfloat16),
            pltpu.VMEM((length // LANES * GROUP, GROUP * STEP), jnp.float32),
            pltpu.VMEM((GROUP, block), jnp.float32),
        ],
        compiler_params=pltpu.CompilerParams(vmem_limit_bytes=VMEM_LIMIT),
    )(groups, slot, row, local, move, weight, waves, wide, scale)
    return scattered(partial_value)


def solution(mesh):
    in_specs = (
        P(("tmpl", "chan"), ("groups", "tm")),
        P(("tmpl", "chan"), "groups"),
        P("tmpl", "chan", None),
        P("tmpl", "chan"),
        P("tmpl", "chan"),
        P("tmpl"),
    )
    out_specs = P(("tmpl", "chan"), ("groups", "tm"))
    return jax.shard_map(body, mesh=mesh, in_specs=in_specs, out_specs=out_specs, check_vma=False)
```

```python
import functools

import jax
import jax.numpy as jnp
from jax import lax
from jax.experimental import pallas as pl
from jax.experimental.pallas import tpu as pltpu
from jax.sharding import PartitionSpec as P

EPS = 1e-06
LANES = 128
GROUP = 8
ROWS = 16
STEP = 32
PIECES = LANES // STEP
VMEM_LIMIT = 60 * 1024 * 1024


def rolled(value, distance):
    size = value.shape[1]
    return pltpu.roll(value, (size - distance) % size, 1)


def window_rows(length, samples_ref, halo, tail_ref, is_last, wide_ref, scale_ref, first, last):
    block, rim = samples_ref.shape[1], tail_ref.shape[1]
    extent, starts = wide_ref.shape[1], scale_ref.shape[1]
    if first == last:
        return

    @pl.loop(first, last)
    def _(i):
        at = pl.ds(pl.multiple_of(i * ROWS, ROWS), ROWS)
        after = jnp.where(is_last, tail_ref[at, :].astype(jnp.float32), halo[at, :].astype(jnp.float32))
        pieces = [samples_ref[at, :].astype(jnp.float32), after]
        if extent > block + rim:
            pieces.append(jnp.zeros((ROWS, extent - block - rim), jnp.float32))
        wide = jnp.concatenate(pieces, axis=1)
        wide_ref[at, :] = wide
        total = wide * wide
        reach = 1
        while reach < LANES:
            total = total + rolled(total, reach)
            reach *= 2
        energy = total[:, :starts]
        for c in range(1, length // LANES):
            energy = energy + total[:, c * LANES : c * LANES + starts]
        scale_ref[at, :] = lax.rsqrt(energy + EPS)


def gather_kernel(
    length, own_ref, code_ref, samples_ref, tail_ref,
    waves_ref, codes_ref, wide_ref, scale_ref,
    halo, halo_sems, code_send, code_recv, z_send, z_recv, x_send, x_recv, c_send, c_recv,
):
    n_z, n_x, n_c = (lax.axis_size(a) for a in ("tmpl", "chan", "tm"))
    z, x, c = (lax.axis_index(a) for a in ("tmpl", "chan", "tm"))
    me = z * n_x + x
    share = own_ref.shape[0] // n_c
    rows = pl.ds(pl.multiple_of(c * share, share), share)
    far = [(k, j) for k in range(n_z) for j in range(n_x) if k or j]

    def ahead(k, j):
        return {"tmpl": lax.rem(z + k, n_z), "chan": lax.rem(x + j, n_x)}

    def sibling(t):
        return {"tm": lax.rem(c + t, n_c)}

    greet([ahead(k, j) for k, j in far] + [sibling(t) for t in range(1, n_c)])
    copies = {}

    def send(name, source, target, send_sem, recv_sem, device):
        copies[name] = pltpu.make_async_remote_copy(
            source, target, send_sem, recv_sem, device_id=device, device_id_type=pl.DeviceIdType.MESH
        )
        copies[name].start()

    def pass_x(k, source, target):
        for j in range(1, n_x):
            send(("x", k, j), source, target, x_send.at[k, j - 1], x_recv.at[k, j - 1], ahead(0, j))

    def pass_core(k, j):
        at = lax.rem(z - k + n_z, n_z) * n_x + lax.rem(x - j + n_x, n_x)
        block = waves_ref.at[at, rows]
        for t in range(1, n_c):
            send(
                ("c", k, j, t), block, block, c_send.at[k * n_x + j, t - 1], c_recv.at[k * n_x + j, t - 1], sibling(t)
            )

    send("halo", samples_ref, halo, halo_sems.at[0], halo_sems.at[1], sibling(n_c - 1))
    for k in range(1, n_z):
        send(("z", k), own_ref.at[rows], waves_ref.at[me, rows], z_send.at[k - 1], z_recv.at[k - 1], ahead(k, 0))
    pass_x(0, own_ref.at[rows], waves_ref.at[me, rows])
    for k, j in far:
        at = k * n_x + j
        send(("code", k, j), code_ref, codes_ref.at[me], code_send.at[at], code_recv.at[at], ahead(k, j))
    waves_ref[me] = own_ref[...]
    codes_ref[me] = code_ref[...]
    copies["halo"].wait_recv()

    steps = samples_ref.shape[0] // ROWS
    marks = [steps * i // (n_z + 1) for i in range(n_z + 2)]
    window = functools.partial(
        window_rows, length, samples_ref, halo, tail_ref, c == n_c - 1, wide_ref, scale_ref
    )
    for k in range(1, n_z):
        window(marks[k - 1], marks[k])
        copies["z", k].wait_recv()
        block = waves_ref.at[lax.rem(z - k + n_z, n_z) * n_x + x, rows]
        pass_x(k, block, block)
        pass_core(k, 0)
    window(marks[n_z - 1], marks[n_z])
    for k in range(n_z):
        for j in range(1, n_x):
            copies["x", k, j].wait_recv()
            pass_core(k, j)
    window(marks[n_z], marks[n_z + 1])
    for k, j in far:
        copies["code", k, j].wait_recv()
        for t in range(1, n_c):
            copies["c", k, j, t].wait_recv()
    for copy in copies.values():
        copy.wait_send()


def detect_kernel(
    layout, number_ref, slot_ref, codes_ref, weight_ref,
    waves_ref, wide_ref, scale_ref, out_ref,
    waves, picked, lined, shifts, spread, own, found,
):
    block = out_ref.shape[1]
    length = waves_ref.shape[1]
    count = length // STEP
    span = shifts.shape[1]
    taken = span + LANES
    scaled = block + LANES
    slots, per_slot, n_chan, per_dev, chans, max_move, max_live = layout
    number = number_ref[0]
    mine = (lax.axis_index("tmpl") * n_chan + lax.axis_index("chan")) * chans

    def place(s):
        code = codes_ref[slot_ref[s]]
        used = s < number
        code = jnp.where(used, code, 0)
        chan = jnp.where(used, lax.div(code, max_move * max_live) - mine, 0)
        move = lax.rem(lax.div(code, max_live), max_move)
        coarse = pl.multiple_of(lax.div(move, LANES) * LANES, LANES)
        return chan, coarse, lax.rem(move, LANES), lax.rem(code, max_live)

    out_ref[...] = jnp.zeros_like(out_ref)

    @pl.loop(0, waves_ref.shape[0] // LANES)
    def _(i):
        at = pl.ds(pl.multiple_of(i * LANES, LANES), LANES)
        waves[at, :] = waves_ref[at, :].astype(jnp.float32)

    width = GROUP * STEP
    k_id = lax.broadcasted_iota(jnp.int32, (LANES, width), 0)
    r_id = lax.broadcasted_iota(jnp.int32, (LANES, width), 1) // GROUP
    for q in range(PIECES):
        spread[:, q * width : (q + 1) * width] = (k_id == r_id + q * STEP).astype(jnp.float32).astype(jnp.bfloat16)
    row_id = lax.broadcasted_iota(jnp.int32, (count // PIECES * GROUP, width), 0) % GROUP
    col_id = lax.broadcasted_iota(jnp.int32, (count // PIECES * GROUP, width), 1) % GROUP
    own[...] = (row_id == col_id).astype(jnp.float32)

    @pl.loop(0, lax.div(number + GROUP - 1, GROUP))
    def _(g):
        for i in range(GROUP):
            s = g * GROUP + i
            chan, coarse, fine, _ = place(s)
            picked[i : i + 1, :] = waves[pl.ds(slot_ref[s], 1), :]
            row = wide_ref[pl.ds(chan, 1), pl.ds(coarse, taken)]
            lined[i : i + 1, :] = pltpu.roll(row, taken - fine, 1)
        wave = picked[...]
        tnorm = lax.rsqrt(jnp.sum(wave * wave, axis=1, keepdims=True) + EPS)
        for r in range(0, STEP, 2):
            pair = [rolled(lined[...], r + k)[:, :span] if r + k else lined[:, :span] for k in range(2)]
            shifts[r * GROUP : (r + 2) * GROUP, :] = jnp.concatenate(pair, axis=0).astype(jnp.bfloat16)
        blocks = count // PIECES
        stacked = jnp.concatenate([wave[:, j * LANES : (j + 1) * LANES] for j in range(blocks)], axis=0)
        expanded = jnp.dot(stacked.astype(jnp.bfloat16), spread[...], preferred_element_type=jnp.float32)
        mask = own[...]
        left = jnp.concatenate([expanded[:, q * width : (q + 1) * width] * mask for q in range(PIECES)], axis=0)
        product = jnp.dot(left.astype(jnp.bfloat16), shifts[...], preferred_element_type=jnp.float32)
        total = None
        for q in range(PIECES):
            part = None
            for j in range(blocks):
                at = (q * blocks + j) * GROUP
                term = product[at : at + GROUP, j * LANES : j * LANES + scaled]
                part = term if part is None else part + term
            if q:
                part = rolled(part, q * STEP)
            total = part if total is None else total + part
        found[...] = total[:, :block] * tnorm
        for i in range(GROUP):
            s = g * GROUP + i
            chan, coarse, fine, live = place(s)
            scale = scale_ref[pl.ds(chan, 1), pl.ds(coarse, scaled)]
            scale = pltpu.roll(scale, scaled - fine, 1)[:, :block]
            slot = slot_ref[s]
            owner = lax.div(slot, slots)
            row = lax.div(owner, n_chan) * per_dev + lax.div(lax.rem(slot, slots), per_slot)
            at = pl.ds(row, 1)
            weight = jnp.where(s < number, weight_ref[live], 0.0)
            out_ref[at, :] += found[i : i + 1, :] * scale * weight


def greet(peers):
    barrier = pltpu.get_barrier_semaphore()
    for peer in peers:
        pl.semaphore_signal(barrier, inc=1, device_id=peer, device_id_type=pl.DeviceIdType.MESH)
    pl.semaphore_wait(barrier, len(peers))


def scatter_kernel(value_ref, out_ref, across, sums, along, x_send, x_recv, z_send, z_recv):
    n_z, n_x = lax.axis_size("tmpl"), lax.axis_size("chan")
    z, x = lax.axis_index("tmpl"), lax.axis_index("chan")
    x_peers = [{"chan": lax.rem(x + j, n_x)} for j in range(1, n_x)]
    z_peers = [{"tmpl": lax.rem(z + k, n_z)} for k in range(1, n_z)]
    greet(x_peers + z_peers)
    order = [*range(1, n_z), 0]
    copies = {}
    for k in order:
        for j in range(1, n_x):
            there = lax.rem(z + k, n_z) * n_x + lax.rem(x + j, n_x)
            copies["x", k, j] = pltpu.make_async_remote_copy(
                value_ref.at[there], across.at[k, j - 1], x_send.at[k, j - 1], x_recv.at[k, j - 1],
                device_id=x_peers[j - 1], device_id_type=pl.DeviceIdType.MESH,
            )
            copies["x", k, j].start()
    for k in order:
        total = value_ref[lax.rem(z + k, n_z) * n_x + x]
        for j in range(1, n_x):
            copies["x", k, j].wait_recv()
            total = total + across[k, j - 1]
        sums[k] = total
        if k:
            copies["z", k] = pltpu.make_async_remote_copy(
                sums.at[k], along.at[k - 1], z_send.at[k - 1], z_recv.at[k - 1],
                device_id=z_peers[k - 1], device_id_type=pl.DeviceIdType.MESH,
            )
            copies["z", k].start()
    total = sums[0]
    for k in range(1, n_z):
        copies["z", k].wait_recv()
        total = total + along[k - 1]
    out_ref[...] = total
    for copy in copies.values():
        copy.wait_send()


def scattered(value):
    n_z, n_x = lax.axis_size("tmpl"), lax.axis_size("chan")
    keep, block = value.shape[0] // (n_z * n_x), value.shape[1]
    return pl.pallas_call(
        scatter_kernel,
        out_shape=jax.ShapeDtypeStruct((keep, block), jnp.float32),
        in_specs=[vmem()],
        out_specs=vmem(),
        scratch_shapes=[
            pltpu.VMEM((n_z, n_x - 1, keep, block), jnp.float32),
            pltpu.VMEM((n_z, keep, block), jnp.float32),
            pltpu.VMEM((n_z - 1, keep, block), jnp.float32),
            pltpu.SemaphoreType.DMA((n_z, n_x - 1)),
            pltpu.SemaphoreType.DMA((n_z, n_x - 1)),
            pltpu.SemaphoreType.DMA((n_z - 1,)),
            pltpu.SemaphoreType.DMA((n_z - 1,)),
        ],
        compiler_params=pltpu.CompilerParams(
            collective_id=1, has_side_effects=True, vmem_limit_bytes=VMEM_LIMIT
        ),
    )(value.reshape(n_z * n_x, keep, block))


def vmem():
    return pl.BlockSpec(memory_space=pltpu.VMEM)


def smem():
    return pl.BlockSpec(memory_space=pltpu.SMEM)


def up(value, multiple):
    return -(-value // multiple) * multiple


def body(samples, tail, templates, channels, moveouts, live):
    chans, block = samples.shape
    per_dev, per_slot, length = templates.shape
    slots = per_dev * per_slot
    n_chan = lax.axis_size("chan")
    parts = lax.axis_size("tmpl") * n_chan
    me = lax.axis_index("tmpl") * n_chan + lax.axis_index("chan")
    n_rows = per_dev * lax.axis_size("tmpl")
    max_live, max_move = 64, 512

    slot_index = lax.axis_index("chan") * per_slot + jnp.arange(per_slot)
    code = (channels * max_move + moveouts) * max_live + live[:, None]
    code = jnp.where(slot_index[None, :] < live[:, None], code, -1).reshape(slots)
    waveform = templates.reshape(slots, length)
    padded = up(chans, ROWS)
    if padded != chans:
        samples = jnp.pad(samples, ((0, padded - chans), (0, 0)))
        tail = jnp.pad(tail, ((0, padded - chans), (0, 0)))
    starts = block + 3 * LANES
    extent = max(starts + length, block + tail.shape[1])
    n_z, n_c = lax.axis_size("tmpl"), lax.axis_size("tm")

    def sems(*extent):
        return [pltpu.SemaphoreType.DMA(extent)] * 2

    waves, codes, wide, scale = pl.pallas_call(
        functools.partial(gather_kernel, length),
        out_shape=(
            jax.ShapeDtypeStruct((parts, slots, length), jnp.bfloat16),
            jax.ShapeDtypeStruct((parts, 1, slots), jnp.int32),
            jax.ShapeDtypeStruct((padded, extent), jnp.float32),
            jax.ShapeDtypeStruct((padded, starts), jnp.float32),
        ),
        in_specs=[vmem()] * 4,
        out_specs=(vmem(),) * 4,
        scratch_shapes=[
            pltpu.VMEM((padded, block), jnp.bfloat16),
            pltpu.SemaphoreType.DMA((2,)),
            *sems(parts),
            *sems(n_z - 1),
            *sems(n_z, n_chan - 1),
            *sems(parts, n_c - 1),
        ],
        compiler_params=pltpu.CompilerParams(
            collective_id=2, has_side_effects=True, vmem_limit_bytes=VMEM_LIMIT
        ),
    )(waveform, code.reshape(1, slots), samples, tail)
    waves = waves.reshape(parts * slots, length)
    codes = codes.reshape(parts * slots)

    total = parts * slots
    index = jnp.arange(total)
    chan = codes // (max_move * max_live)
    mine = (codes >= 0) & (chan // chans == me)
    before = jnp.sum((index[None, :] < index[:, None]) & mine[None, :], axis=1, dtype=jnp.int32)
    number = jnp.sum(mine, dtype=jnp.int32)
    hit = (before[None, :] == index[:, None]) & mine[None, :]
    slot = jnp.sum(jnp.where(hit, index[None, :], 0), axis=1, dtype=jnp.int32)
    live_f = jnp.maximum(jnp.arange(max_live), 1).astype(jnp.float32)
    weight = jnp.sqrt(jnp.float32(length) / live_f)
    layout = (slots, per_slot, n_chan, per_dev, chans, max_move, max_live)

    span = up(block + length - STEP, LANES)
    partial_value = pl.pallas_call(
        functools.partial(detect_kernel, layout),
        out_shape=jax.ShapeDtypeStruct((n_rows, block), jnp.float32),
        in_specs=[smem()] * 4 + [vmem()] * 3,
        out_specs=vmem(),
        scratch_shapes=[
            pltpu.VMEM((total, length), jnp.float32),
            pltpu.VMEM((GROUP, length), jnp.float32),
            pltpu.VMEM((GROUP, span + LANES), jnp.float32),
            pltpu.VMEM((GROUP * STEP, span), jnp.bfloat16),
            pltpu.VMEM((LANES, PIECES * GROUP * STEP), jnp.bfloat16),
            pltpu.VMEM((length // LANES * GROUP, GROUP * STEP), jnp.float32),
            pltpu.VMEM((GROUP, block), jnp.float32),
        ],
        compiler_params=pltpu.CompilerParams(vmem_limit_bytes=VMEM_LIMIT),
    )(number.reshape(1), slot, codes, weight, waves, wide, scale)
    return scattered(partial_value)


def solution(mesh):
    in_specs = (
        P(("tmpl", "chan"), ("groups", "tm")),
        P(("tmpl", "chan"), "groups"),
        P("tmpl", "chan", None),
        P("tmpl", "chan"),
        P("tmpl", "chan"),
        P("tmpl"),
    )
    out_specs = P(("tmpl", "chan"), ("groups", "tm"))
    return jax.shard_map(body, mesh=mesh, in_specs=in_specs, out_specs=out_specs, check_vma=False)
```

```python
import functools

import jax
import jax.numpy as jnp
from jax import lax
from jax.experimental import pallas as pl
from jax.experimental.pallas import tpu as pltpu
from jax.sharding import PartitionSpec as P

EPS = 1e-06
LANES = 128
GROUP = 8
PAIR = 2
ROWS = 16
STEP = 32
PIECES = LANES // STEP
VMEM_LIMIT = 60 * 1024 * 1024


def rolled(value, distance):
    size = value.shape[1]
    return pltpu.roll(value, (size - distance) % size, 1)


def window_rows(length, samples_ref, halo, tail_ref, is_last, wide_ref, scale_ref, first, last):
    block, rim = samples_ref.shape[1], tail_ref.shape[1]
    extent, starts = wide_ref.shape[1], scale_ref.shape[1]
    if first == last:
        return

    @pl.loop(first, last)
    def _(i):
        at = pl.ds(pl.multiple_of(i * ROWS, ROWS), ROWS)
        after = jnp.where(is_last, tail_ref[at, :].astype(jnp.float32), halo[at, :].astype(jnp.float32))
        pieces = [samples_ref[at, :].astype(jnp.float32), after]
        if extent > block + rim:
            pieces.append(jnp.zeros((ROWS, extent - block - rim), jnp.float32))
        wide = jnp.concatenate(pieces, axis=1)
        wide_ref[at, :] = wide
        total = wide * wide
        reach = 1
        while reach < LANES:
            total = total + rolled(total, reach)
            reach *= 2
        energy = total[:, :starts]
        for c in range(1, length // LANES):
            energy = energy + total[:, c * LANES : c * LANES + starts]
        scale_ref[at, :] = lax.rsqrt(energy + EPS)


def gather_kernel(
    length, own_ref, code_ref, samples_ref, tail_ref,
    waves_ref, codes_ref, wide_ref, scale_ref,
    halo, halo_sems, code_send, code_recv, z_send, z_recv, x_send, x_recv, c_send, c_recv,
):
    n_z, n_x, n_c = (lax.axis_size(a) for a in ("tmpl", "chan", "tm"))
    z, x, c = (lax.axis_index(a) for a in ("tmpl", "chan", "tm"))
    me = z * n_x + x
    share = own_ref.shape[0] // n_c
    rows = pl.ds(pl.multiple_of(c * share, share), share)
    far = [(k, j) for k in range(n_z) for j in range(n_x) if k or j]

    def ahead(k, j):
        return {"tmpl": lax.rem(z + k, n_z), "chan": lax.rem(x + j, n_x)}

    def sibling(t):
        return {"tm": lax.rem(c + t, n_c)}

    greet([ahead(k, j) for k, j in far] + [sibling(t) for t in range(1, n_c)])
    copies = {}

    def send(name, source, target, send_sem, recv_sem, device):
        copies[name] = pltpu.make_async_remote_copy(
            source, target, send_sem, recv_sem, device_id=device, device_id_type=pl.DeviceIdType.MESH
        )
        copies[name].start()

    def pass_x(k, source, target):
        for j in range(1, n_x):
            send(("x", k, j), source, target, x_send.at[k, j - 1], x_recv.at[k, j - 1], ahead(0, j))

    def pass_core(k, j):
        at = lax.rem(z - k + n_z, n_z) * n_x + lax.rem(x - j + n_x, n_x)
        block = waves_ref.at[at, rows]
        for t in range(1, n_c):
            send(
                ("c", k, j, t), block, block, c_send.at[k * n_x + j, t - 1], c_recv.at[k * n_x + j, t - 1], sibling(t)
            )

    send("halo", samples_ref, halo, halo_sems.at[0], halo_sems.at[1], sibling(n_c - 1))
    for k in range(1, n_z):
        send(("z", k), own_ref.at[rows], waves_ref.at[me, rows], z_send.at[k - 1], z_recv.at[k - 1], ahead(k, 0))
    pass_x(0, own_ref.at[rows], waves_ref.at[me, rows])
    for k, j in far:
        at = k * n_x + j
        send(("code", k, j), code_ref, codes_ref.at[me], code_send.at[at], code_recv.at[at], ahead(k, j))
    waves_ref[me] = own_ref[...]
    codes_ref[me] = code_ref[...]
    copies["halo"].wait_recv()

    steps = samples_ref.shape[0] // ROWS
    marks = [steps * i // (n_z + 1) for i in range(n_z + 2)]
    window = functools.partial(
        window_rows, length, samples_ref, halo, tail_ref, c == n_c - 1, wide_ref, scale_ref
    )
    for k in range(1, n_z):
        window(marks[k - 1], marks[k])
        copies["z", k].wait_recv()
        block = waves_ref.at[lax.rem(z - k + n_z, n_z) * n_x + x, rows]
        pass_x(k, block, block)
        pass_core(k, 0)
    window(marks[n_z - 1], marks[n_z])
    for k in range(n_z):
        for j in range(1, n_x):
            copies["x", k, j].wait_recv()
            pass_core(k, j)
    window(marks[n_z], marks[n_z + 1])
    for k, j in far:
        copies["code", k, j].wait_recv()
        for t in range(1, n_c):
            copies["c", k, j, t].wait_recv()
    for copy in copies.values():
        copy.wait_send()


def detect_kernel(
    layout, number_ref, slot_ref, codes_ref, weight_ref,
    waves_ref, wide_ref, scale_ref, out_ref,
    waves, picked, lined, shifts, spread, own, found,
):
    block = out_ref.shape[1]
    length = waves_ref.shape[1]
    count = length // STEP
    span = shifts.shape[2]
    taken = span + LANES
    scaled = block + LANES
    slots, per_slot, n_chan, per_dev, chans, max_move, max_live = layout
    number = number_ref[0]
    mine = (lax.axis_index("tmpl") * n_chan + lax.axis_index("chan")) * chans

    def place(s):
        code = codes_ref[slot_ref[s]]
        used = s < number
        code = jnp.where(used, code, 0)
        chan = jnp.where(used, lax.div(code, max_move * max_live) - mine, 0)
        move = lax.rem(lax.div(code, max_live), max_move)
        coarse = pl.multiple_of(lax.div(move, LANES) * LANES, LANES)
        return chan, coarse, lax.rem(move, LANES), lax.rem(code, max_live)

    out_ref[...] = jnp.zeros_like(out_ref)

    @pl.loop(0, waves_ref.shape[0] // LANES)
    def _(i):
        at = pl.ds(pl.multiple_of(i * LANES, LANES), LANES)
        waves[at, :] = waves_ref[at, :].astype(jnp.float32)

    width = GROUP * STEP
    k_id = lax.broadcasted_iota(jnp.int32, (LANES, width), 0)
    r_id = lax.broadcasted_iota(jnp.int32, (LANES, width), 1) // GROUP
    for q in range(PIECES):
        spread[:, q * width : (q + 1) * width] = (k_id == r_id + q * STEP).astype(jnp.float32).astype(jnp.bfloat16)
    row_id = lax.broadcasted_iota(jnp.int32, (count // PIECES * GROUP, width), 0) % GROUP
    col_id = lax.broadcasted_iota(jnp.int32, (count // PIECES * GROUP, width), 1) % GROUP
    own[...] = (row_id == col_id).astype(jnp.float32)

    @pl.loop(0, lax.div(number + PAIR * GROUP - 1, PAIR * GROUP))
    def _(g):
        for u in range(PAIR):
            first = (g * PAIR + u) * GROUP
            picked_u, lined_u, shifts_u, found_u = picked.at[u], lined.at[u], shifts.at[u], found.at[u]
            for i in range(GROUP):
                s = first + i
                chan, coarse, fine, _ = place(s)
                picked_u[i : i + 1, :] = waves[pl.ds(slot_ref[s], 1), :]
                row = wide_ref[pl.ds(chan, 1), pl.ds(coarse, taken)]
                lined_u[i : i + 1, :] = pltpu.roll(row, taken - fine, 1)
        for u in range(PAIR):
            first = (g * PAIR + u) * GROUP
            picked_u, lined_u, shifts_u, found_u = picked.at[u], lined.at[u], shifts.at[u], found.at[u]
            wave = picked_u[...]
            tnorm = lax.rsqrt(jnp.sum(wave * wave, axis=1, keepdims=True) + EPS)
            for r in range(0, STEP, 2):
                pair = [rolled(lined_u[...], r + k)[:, :span] if r + k else lined_u[:, :span] for k in range(2)]
                shifts_u[r * GROUP : (r + 2) * GROUP, :] = jnp.concatenate(pair, axis=0).astype(jnp.bfloat16)
            blocks = count // PIECES
            stacked = jnp.concatenate([wave[:, j * LANES : (j + 1) * LANES] for j in range(blocks)], axis=0)
            expanded = jnp.dot(stacked.astype(jnp.bfloat16), spread[...], preferred_element_type=jnp.float32)
            mask = own[...]
            left = jnp.concatenate([expanded[:, q * width : (q + 1) * width] * mask for q in range(PIECES)], axis=0)
            product = jnp.dot(left.astype(jnp.bfloat16), shifts_u[...], preferred_element_type=jnp.float32)
            total = None
            for q in range(PIECES):
                part = None
                for j in range(blocks):
                    at = (q * blocks + j) * GROUP
                    term = product[at : at + GROUP, j * LANES : j * LANES + scaled]
                    part = term if part is None else part + term
                if q:
                    part = rolled(part, q * STEP)
                total = part if total is None else total + part
            found_u[...] = total[:, :block] * tnorm
        for u in range(PAIR):
            first = (g * PAIR + u) * GROUP
            picked_u, lined_u, shifts_u, found_u = picked.at[u], lined.at[u], shifts.at[u], found.at[u]
            for i in range(GROUP):
                s = first + i
                chan, coarse, fine, live = place(s)
                scale = scale_ref[pl.ds(chan, 1), pl.ds(coarse, scaled)]
                scale = pltpu.roll(scale, scaled - fine, 1)[:, :block]
                slot = slot_ref[s]
                owner = lax.div(slot, slots)
                row = lax.div(owner, n_chan) * per_dev + lax.div(lax.rem(slot, slots), per_slot)
                at = pl.ds(row, 1)
                weight = jnp.where(s < number, weight_ref[live], 0.0)
                out_ref[at, :] += found_u[i : i + 1, :] * scale * weight


def greet(peers):
    barrier = pltpu.get_barrier_semaphore()
    for peer in peers:
        pl.semaphore_signal(barrier, inc=1, device_id=peer, device_id_type=pl.DeviceIdType.MESH)
    pl.semaphore_wait(barrier, len(peers))


def scatter_kernel(value_ref, out_ref, across, sums, along, x_send, x_recv, z_send, z_recv):
    n_z, n_x = lax.axis_size("tmpl"), lax.axis_size("chan")
    z, x = lax.axis_index("tmpl"), lax.axis_index("chan")
    x_peers = [{"chan": lax.rem(x + j, n_x)} for j in range(1, n_x)]
    z_peers = [{"tmpl": lax.rem(z + k, n_z)} for k in range(1, n_z)]
    greet(x_peers + z_peers)
    order = [*range(1, n_z), 0]
    copies = {}
    for k in order:
        for j in range(1, n_x):
            there = lax.rem(z + k, n_z) * n_x + lax.rem(x + j, n_x)
            copies["x", k, j] = pltpu.make_async_remote_copy(
                value_ref.at[there], across.at[k, j - 1], x_send.at[k, j - 1], x_recv.at[k, j - 1],
                device_id=x_peers[j - 1], device_id_type=pl.DeviceIdType.MESH,
            )
            copies["x", k, j].start()
    for k in order:
        total = value_ref[lax.rem(z + k, n_z) * n_x + x]
        for j in range(1, n_x):
            copies["x", k, j].wait_recv()
            total = total + across[k, j - 1]
        sums[k] = total
        if k:
            copies["z", k] = pltpu.make_async_remote_copy(
                sums.at[k], along.at[k - 1], z_send.at[k - 1], z_recv.at[k - 1],
                device_id=z_peers[k - 1], device_id_type=pl.DeviceIdType.MESH,
            )
            copies["z", k].start()
    total = sums[0]
    for k in range(1, n_z):
        copies["z", k].wait_recv()
        total = total + along[k - 1]
    out_ref[...] = total
    for copy in copies.values():
        copy.wait_send()


def scattered(value):
    n_z, n_x = lax.axis_size("tmpl"), lax.axis_size("chan")
    keep, block = value.shape[0] // (n_z * n_x), value.shape[1]
    return pl.pallas_call(
        scatter_kernel,
        out_shape=jax.ShapeDtypeStruct((keep, block), jnp.float32),
        in_specs=[vmem()],
        out_specs=vmem(),
        scratch_shapes=[
            pltpu.VMEM((n_z, n_x - 1, keep, block), jnp.float32),
            pltpu.VMEM((n_z, keep, block), jnp.float32),
            pltpu.VMEM((n_z - 1, keep, block), jnp.float32),
            pltpu.SemaphoreType.DMA((n_z, n_x - 1)),
            pltpu.SemaphoreType.DMA((n_z, n_x - 1)),
            pltpu.SemaphoreType.DMA((n_z - 1,)),
            pltpu.SemaphoreType.DMA((n_z - 1,)),
        ],
        compiler_params=pltpu.CompilerParams(
            collective_id=1, has_side_effects=True, vmem_limit_bytes=VMEM_LIMIT
        ),
    )(value.reshape(n_z * n_x, keep, block))


def vmem():
    return pl.BlockSpec(memory_space=pltpu.VMEM)


def smem():
    return pl.BlockSpec(memory_space=pltpu.SMEM)


def up(value, multiple):
    return -(-value // multiple) * multiple


def body(samples, tail, templates, channels, moveouts, live):
    chans, block = samples.shape
    per_dev, per_slot, length = templates.shape
    slots = per_dev * per_slot
    n_chan = lax.axis_size("chan")
    parts = lax.axis_size("tmpl") * n_chan
    me = lax.axis_index("tmpl") * n_chan + lax.axis_index("chan")
    n_rows = per_dev * lax.axis_size("tmpl")
    max_live, max_move = 64, 512

    slot_index = lax.axis_index("chan") * per_slot + jnp.arange(per_slot)
    code = (channels * max_move + moveouts) * max_live + live[:, None]
    code = jnp.where(slot_index[None, :] < live[:, None], code, -1).reshape(slots)
    waveform = templates.reshape(slots, length)
    padded = up(chans, ROWS)
    if padded != chans:
        samples = jnp.pad(samples, ((0, padded - chans), (0, 0)))
        tail = jnp.pad(tail, ((0, padded - chans), (0, 0)))
    starts = block + 3 * LANES
    extent = max(starts + length, block + tail.shape[1])
    n_z, n_c = lax.axis_size("tmpl"), lax.axis_size("tm")

    def sems(*extent):
        return [pltpu.SemaphoreType.DMA(extent)] * 2

    waves, codes, wide, scale = pl.pallas_call(
        functools.partial(gather_kernel, length),
        out_shape=(
            jax.ShapeDtypeStruct((parts, slots, length), jnp.bfloat16),
            jax.ShapeDtypeStruct((parts, 1, slots), jnp.int32),
            jax.ShapeDtypeStruct((padded, extent), jnp.float32),
            jax.ShapeDtypeStruct((padded, starts), jnp.float32),
        ),
        in_specs=[vmem()] * 4,
        out_specs=(vmem(),) * 4,
        scratch_shapes=[
            pltpu.VMEM((padded, block), jnp.bfloat16),
            pltpu.SemaphoreType.DMA((2,)),
            *sems(parts),
            *sems(n_z - 1),
            *sems(n_z, n_chan - 1),
            *sems(parts, n_c - 1),
        ],
        compiler_params=pltpu.CompilerParams(
            collective_id=2, has_side_effects=True, vmem_limit_bytes=VMEM_LIMIT
        ),
    )(waveform, code.reshape(1, slots), samples, tail)
    waves = waves.reshape(parts * slots, length)
    codes = codes.reshape(parts * slots)

    total = parts * slots
    index = jnp.arange(total)
    chan = codes // (max_move * max_live)
    mine = (codes >= 0) & (chan // chans == me)
    before = jnp.sum((index[None, :] < index[:, None]) & mine[None, :], axis=1, dtype=jnp.int32)
    number = jnp.sum(mine, dtype=jnp.int32)
    hit = (before[None, :] == index[:, None]) & mine[None, :]
    slot = jnp.sum(jnp.where(hit, index[None, :], 0), axis=1, dtype=jnp.int32)
    live_f = jnp.maximum(jnp.arange(max_live), 1).astype(jnp.float32)
    weight = jnp.sqrt(jnp.float32(length) / live_f)
    layout = (slots, per_slot, n_chan, per_dev, chans, max_move, max_live)

    span = up(block + length - STEP, LANES)
    partial_value = pl.pallas_call(
        functools.partial(detect_kernel, layout),
        out_shape=jax.ShapeDtypeStruct((n_rows, block), jnp.float32),
        in_specs=[smem()] * 4 + [vmem()] * 3,
        out_specs=vmem(),
        scratch_shapes=[
            pltpu.VMEM((total, length), jnp.float32),
            pltpu.VMEM((PAIR, GROUP, length), jnp.float32),
            pltpu.VMEM((PAIR, GROUP, span + LANES), jnp.float32),
            pltpu.VMEM((PAIR, GROUP * STEP, span), jnp.bfloat16),
            pltpu.VMEM((LANES, PIECES * GROUP * STEP), jnp.bfloat16),
            pltpu.VMEM((length // LANES * GROUP, GROUP * STEP), jnp.float32),
            pltpu.VMEM((PAIR, GROUP, block), jnp.float32),
        ],
        compiler_params=pltpu.CompilerParams(vmem_limit_bytes=VMEM_LIMIT),
    )(number.reshape(1), slot, codes, weight, waves, wide, scale)
    return scattered(partial_value)


def solution(mesh):
    in_specs = (
        P(("tmpl", "chan"), ("groups", "tm")),
        P(("tmpl", "chan"), "groups"),
        P("tmpl", "chan", None),
        P("tmpl", "chan"),
        P("tmpl", "chan"),
        P("tmpl"),
    )
    out_specs = P(("tmpl", "chan"), ("groups", "tm"))
    return jax.shard_map(body, mesh=mesh, in_specs=in_specs, out_specs=out_specs, check_vma=False)
```

```python
import functools

import jax
import jax.numpy as jnp
from jax import lax
from jax.experimental import pallas as pl
from jax.experimental.pallas import tpu as pltpu
from jax.sharding import PartitionSpec as P

EPS = 1e-06
LANES = 128
GROUP = 8
ROWS = 16
STEP = 32
PIECES = LANES // STEP
VMEM_LIMIT = 60 * 1024 * 1024


def rolled(value, distance):
    size = value.shape[1]
    return pltpu.roll(value, (size - distance) % size, 1)


def window_rows(length, samples_ref, halo, tail_ref, is_last, wide_ref, scale_ref, first, last):
    block, rim = samples_ref.shape[1], tail_ref.shape[1]
    extent, starts = wide_ref.shape[1], scale_ref.shape[1]
    if first == last:
        return

    @pl.loop(first, last)
    def _(i):
        at = pl.ds(pl.multiple_of(i * ROWS, ROWS), ROWS)
        after = jnp.where(is_last, tail_ref[at, :].astype(jnp.float32), halo[at, :].astype(jnp.float32))
        pieces = [samples_ref[at, :].astype(jnp.float32), after]
        if extent > block + rim:
            pieces.append(jnp.zeros((ROWS, extent - block - rim), jnp.float32))
        wide = jnp.concatenate(pieces, axis=1)
        wide_ref[at, :] = wide
        total = wide * wide
        reach = 1
        while reach < LANES:
            total = total + rolled(total, reach)
            reach *= 2
        energy = total[:, :starts]
        for c in range(1, length // LANES):
            energy = energy + total[:, c * LANES : c * LANES + starts]
        scale_ref[at, :] = lax.rsqrt(energy + EPS)


def gather_kernel(
    length, own_ref, code_ref, samples_ref, tail_ref,
    waves_ref, codes_ref, wide_ref, scale_ref,
    halo, halo_sems, code_send, code_recv, z_send, z_recv, x_send, x_recv, c_send, c_recv,
):
    n_z, n_x, n_c = (lax.axis_size(a) for a in ("tmpl", "chan", "tm"))
    z, x, c = (lax.axis_index(a) for a in ("tmpl", "chan", "tm"))
    me = z * n_x + x
    share = own_ref.shape[0] // n_c
    rows = pl.ds(pl.multiple_of(c * share, share), share)
    far = [(k, j) for k in range(n_z) for j in range(n_x) if k or j]

    def ahead(k, j):
        return {"tmpl": lax.rem(z + k, n_z), "chan": lax.rem(x + j, n_x)}

    def sibling(t):
        return {"tm": lax.rem(c + t, n_c)}

    greet([ahead(k, j) for k, j in far] + [sibling(t) for t in range(1, n_c)])
    copies = {}

    def send(name, source, target, send_sem, recv_sem, device):
        copies[name] = pltpu.make_async_remote_copy(
            source, target, send_sem, recv_sem, device_id=device, device_id_type=pl.DeviceIdType.MESH
        )
        copies[name].start()

    def pass_x(k, source, target):
        for j in range(1, n_x):
            send(("x", k, j), source, target, x_send.at[k, j - 1], x_recv.at[k, j - 1], ahead(0, j))

    def pass_core(k, j):
        at = lax.rem(z - k + n_z, n_z) * n_x + lax.rem(x - j + n_x, n_x)
        block = waves_ref.at[at, rows]
        for t in range(1, n_c):
            send(
                ("c", k, j, t), block, block, c_send.at[k * n_x + j, t - 1], c_recv.at[k * n_x + j, t - 1], sibling(t)
            )

    send("halo", samples_ref, halo, halo_sems.at[0], halo_sems.at[1], sibling(n_c - 1))
    for k in range(1, n_z):
        send(("z", k), own_ref.at[rows], waves_ref.at[me, rows], z_send.at[k - 1], z_recv.at[k - 1], ahead(k, 0))
    pass_x(0, own_ref.at[rows], waves_ref.at[me, rows])
    for k, j in far:
        at = k * n_x + j
        send(("code", k, j), code_ref, codes_ref.at[me], code_send.at[at], code_recv.at[at], ahead(k, j))
    waves_ref[me] = own_ref[...]
    codes_ref[me] = code_ref[...]
    copies["halo"].wait_recv()

    steps = samples_ref.shape[0] // ROWS
    marks = [steps * i // (n_z + 1) for i in range(n_z + 2)]
    window = functools.partial(
        window_rows, length, samples_ref, halo, tail_ref, c == n_c - 1, wide_ref, scale_ref
    )
    for k in range(1, n_z):
        window(marks[k - 1], marks[k])
        copies["z", k].wait_recv()
        block = waves_ref.at[lax.rem(z - k + n_z, n_z) * n_x + x, rows]
        pass_x(k, block, block)
        pass_core(k, 0)
    window(marks[n_z - 1], marks[n_z])
    for k in range(n_z):
        for j in range(1, n_x):
            copies["x", k, j].wait_recv()
            pass_core(k, j)
    window(marks[n_z], marks[n_z + 1])
    for k, j in far:
        copies["code", k, j].wait_recv()
        for t in range(1, n_c):
            copies["c", k, j, t].wait_recv()
    for copy in copies.values():
        copy.wait_send()


def quotient(value, by):
    return value >> (by.bit_length() - 1) if by & (by - 1) == 0 else lax.div(value, by)


def remainder(value, by):
    return value & (by - 1) if by & (by - 1) == 0 else lax.rem(value, by)


def detect_kernel(
    layout, number_ref, slot_ref, codes_ref, weight_ref,
    waves_ref, wide_ref, scale_ref, out_ref,
    waves, picked, lined, shifts, spread, own, found,
):
    block = out_ref.shape[1]
    length = waves_ref.shape[1]
    count = length // STEP
    span = shifts.shape[1]
    taken = span + LANES
    scaled = block + LANES
    slots, per_slot, n_chan, per_dev, chans, max_move, max_live = layout
    number = number_ref[0]
    mine = (lax.axis_index("tmpl") * n_chan + lax.axis_index("chan")) * chans

    def place(s):
        code = codes_ref[slot_ref[s]]
        used = s < number
        code = jnp.where(used, code, 0)
        chan = jnp.where(used, quotient(code, max_move * max_live) - mine, 0)
        move = remainder(quotient(code, max_live), max_move)
        coarse = pl.multiple_of(quotient(move, LANES) * LANES, LANES)
        return chan, coarse, remainder(move, LANES), remainder(code, max_live)

    out_ref[...] = jnp.zeros_like(out_ref)

    @pl.loop(0, waves_ref.shape[0] // LANES)
    def _(i):
        at = pl.ds(pl.multiple_of(i * LANES, LANES), LANES)
        waves[at, :] = waves_ref[at, :].astype(jnp.float32)

    width = GROUP * STEP
    k_id = lax.broadcasted_iota(jnp.int32, (LANES, width), 0)
    r_id = lax.broadcasted_iota(jnp.int32, (LANES, width), 1) // GROUP
    for q in range(PIECES):
        spread[:, q * width : (q + 1) * width] = (k_id == r_id + q * STEP).astype(jnp.float32).astype(jnp.bfloat16)
    row_id = lax.broadcasted_iota(jnp.int32, (count // PIECES * GROUP, width), 0) % GROUP
    col_id = lax.broadcasted_iota(jnp.int32, (count // PIECES * GROUP, width), 1) % GROUP
    own[...] = (row_id == col_id).astype(jnp.float32)

    @pl.loop(0, quotient(number + GROUP - 1, GROUP))
    def _(g):
        places = []
        for i in range(GROUP):
            s = g * GROUP + i
            places.append(place(s))
            chan, coarse, fine, _ = places[i]
            picked[i : i + 1, :] = waves[pl.ds(slot_ref[s], 1), :]
            row = wide_ref[pl.ds(chan, 1), pl.ds(coarse, taken)]
            lined[i : i + 1, :] = pltpu.roll(row, taken - fine, 1)
        wave = picked[...]
        tnorm = lax.rsqrt(jnp.sum(wave * wave, axis=1, keepdims=True) + EPS)
        for r in range(0, STEP, 2):
            pair = [rolled(lined[...], r + k)[:, :span] if r + k else lined[:, :span] for k in range(2)]
            shifts[r * GROUP : (r + 2) * GROUP, :] = jnp.concatenate(pair, axis=0).astype(jnp.bfloat16)
        blocks = count // PIECES
        stacked = jnp.concatenate([wave[:, j * LANES : (j + 1) * LANES] for j in range(blocks)], axis=0)
        expanded = jnp.dot(stacked.astype(jnp.bfloat16), spread[...], preferred_element_type=jnp.float32)
        mask = own[...]
        left = jnp.concatenate([expanded[:, q * width : (q + 1) * width] * mask for q in range(PIECES)], axis=0)
        product = jnp.dot(left.astype(jnp.bfloat16), shifts[...], preferred_element_type=jnp.float32)
        total = None
        for q in range(PIECES):
            part = None
            for j in range(blocks):
                at = (q * blocks + j) * GROUP
                term = product[at : at + GROUP, j * LANES : j * LANES + scaled]
                part = term if part is None else part + term
            if q:
                part = rolled(part, q * STEP)
            total = part if total is None else total + part
        found[...] = total[:, :block] * tnorm
        for i in range(GROUP):
            s = g * GROUP + i
            chan, coarse, fine, live = places[i]
            scale = scale_ref[pl.ds(chan, 1), pl.ds(coarse, scaled)]
            scale = pltpu.roll(scale, scaled - fine, 1)[:, :block]
            slot = slot_ref[s]
            owner = quotient(slot, slots)
            row = quotient(owner, n_chan) * per_dev + quotient(remainder(slot, slots), per_slot)
            at = pl.ds(row, 1)
            weight = jnp.where(s < number, weight_ref[live], 0.0)
            out_ref[at, :] += found[i : i + 1, :] * scale * weight


def greet(peers):
    barrier = pltpu.get_barrier_semaphore()
    for peer in peers:
        pl.semaphore_signal(barrier, inc=1, device_id=peer, device_id_type=pl.DeviceIdType.MESH)
    pl.semaphore_wait(barrier, len(peers))


def scatter_kernel(value_ref, out_ref, across, sums, along, x_send, x_recv, z_send, z_recv):
    n_z, n_x = lax.axis_size("tmpl"), lax.axis_size("chan")
    z, x = lax.axis_index("tmpl"), lax.axis_index("chan")
    x_peers = [{"chan": lax.rem(x + j, n_x)} for j in range(1, n_x)]
    z_peers = [{"tmpl": lax.rem(z + k, n_z)} for k in range(1, n_z)]
    greet(x_peers + z_peers)
    order = [*range(1, n_z), 0]
    copies = {}
    for k in order:
        for j in range(1, n_x):
            there = lax.rem(z + k, n_z) * n_x + lax.rem(x + j, n_x)
            copies["x", k, j] = pltpu.make_async_remote_copy(
                value_ref.at[there], across.at[k, j - 1], x_send.at[k, j - 1], x_recv.at[k, j - 1],
                device_id=x_peers[j - 1], device_id_type=pl.DeviceIdType.MESH,
            )
            copies["x", k, j].start()
    for k in order:
        total = value_ref[lax.rem(z + k, n_z) * n_x + x]
        for j in range(1, n_x):
            copies["x", k, j].wait_recv()
            total = total + across[k, j - 1]
        sums[k] = total
        if k:
            copies["z", k] = pltpu.make_async_remote_copy(
                sums.at[k], along.at[k - 1], z_send.at[k - 1], z_recv.at[k - 1],
                device_id=z_peers[k - 1], device_id_type=pl.DeviceIdType.MESH,
            )
            copies["z", k].start()
    total = sums[0]
    for k in range(1, n_z):
        copies["z", k].wait_recv()
        total = total + along[k - 1]
    out_ref[...] = total
    for copy in copies.values():
        copy.wait_send()


def scattered(value):
    n_z, n_x = lax.axis_size("tmpl"), lax.axis_size("chan")
    keep, block = value.shape[0] // (n_z * n_x), value.shape[1]
    return pl.pallas_call(
        scatter_kernel,
        out_shape=jax.ShapeDtypeStruct((keep, block), jnp.float32),
        in_specs=[vmem()],
        out_specs=vmem(),
        scratch_shapes=[
            pltpu.VMEM((n_z, n_x - 1, keep, block), jnp.float32),
            pltpu.VMEM((n_z, keep, block), jnp.float32),
            pltpu.VMEM((n_z - 1, keep, block), jnp.float32),
            pltpu.SemaphoreType.DMA((n_z, n_x - 1)),
            pltpu.SemaphoreType.DMA((n_z, n_x - 1)),
            pltpu.SemaphoreType.DMA((n_z - 1,)),
            pltpu.SemaphoreType.DMA((n_z - 1,)),
        ],
        compiler_params=pltpu.CompilerParams(
            collective_id=1, has_side_effects=True, vmem_limit_bytes=VMEM_LIMIT
        ),
    )(value.reshape(n_z * n_x, keep, block))


def vmem():
    return pl.BlockSpec(memory_space=pltpu.VMEM)


def smem():
    return pl.BlockSpec(memory_space=pltpu.SMEM)


def up(value, multiple):
    return -(-value // multiple) * multiple


def body(samples, tail, templates, channels, moveouts, live):
    chans, block = samples.shape
    per_dev, per_slot, length = templates.shape
    slots = per_dev * per_slot
    n_chan = lax.axis_size("chan")
    parts = lax.axis_size("tmpl") * n_chan
    me = lax.axis_index("tmpl") * n_chan + lax.axis_index("chan")
    n_rows = per_dev * lax.axis_size("tmpl")
    max_live, max_move = 64, 512

    slot_index = lax.axis_index("chan") * per_slot + jnp.arange(per_slot)
    code = (channels * max_move + moveouts) * max_live + live[:, None]
    code = jnp.where(slot_index[None, :] < live[:, None], code, -1).reshape(slots)
    waveform = templates.reshape(slots, length)
    padded = up(chans, ROWS)
    if padded != chans:
        samples = jnp.pad(samples, ((0, padded - chans), (0, 0)))
        tail = jnp.pad(tail, ((0, padded - chans), (0, 0)))
    starts = block + 3 * LANES
    extent = max(starts + length, block + tail.shape[1])
    n_z, n_c = lax.axis_size("tmpl"), lax.axis_size("tm")

    def sems(*extent):
        return [pltpu.SemaphoreType.DMA(extent)] * 2

    waves, codes, wide, scale = pl.pallas_call(
        functools.partial(gather_kernel, length),
        out_shape=(
            jax.ShapeDtypeStruct((parts, slots, length), jnp.bfloat16),
            jax.ShapeDtypeStruct((parts, 1, slots), jnp.int32),
            jax.ShapeDtypeStruct((padded, extent), jnp.float32),
            jax.ShapeDtypeStruct((padded, starts), jnp.float32),
        ),
        in_specs=[vmem()] * 4,
        out_specs=(vmem(),) * 4,
        scratch_shapes=[
            pltpu.VMEM((padded, block), jnp.bfloat16),
            pltpu.SemaphoreType.DMA((2,)),
            *sems(parts),
            *sems(n_z - 1),
            *sems(n_z, n_chan - 1),
            *sems(parts, n_c - 1),
        ],
        compiler_params=pltpu.CompilerParams(
            collective_id=2, has_side_effects=True, vmem_limit_bytes=VMEM_LIMIT
        ),
    )(waveform, code.reshape(1, slots), samples, tail)
    waves = waves.reshape(parts * slots, length)
    codes = codes.reshape(parts * slots)

    total = parts * slots
    index = jnp.arange(total)
    chan = codes // (max_move * max_live)
    mine = (codes >= 0) & (chan // chans == me)
    before = jnp.sum((index[None, :] < index[:, None]) & mine[None, :], axis=1, dtype=jnp.int32)
    number = jnp.sum(mine, dtype=jnp.int32)
    hit = (before[None, :] == index[:, None]) & mine[None, :]
    slot = jnp.sum(jnp.where(hit, index[None, :], 0), axis=1, dtype=jnp.int32)
    live_f = jnp.maximum(jnp.arange(max_live), 1).astype(jnp.float32)
    weight = jnp.sqrt(jnp.float32(length) / live_f)
    layout = (slots, per_slot, n_chan, per_dev, chans, max_move, max_live)

    span = up(block + length - STEP, LANES)
    partial_value = pl.pallas_call(
        functools.partial(detect_kernel, layout),
        out_shape=jax.ShapeDtypeStruct((n_rows, block), jnp.float32),
        in_specs=[smem()] * 4 + [vmem()] * 3,
        out_specs=vmem(),
        scratch_shapes=[
            pltpu.VMEM((total, length), jnp.float32),
            pltpu.VMEM((GROUP, length), jnp.float32),
            pltpu.VMEM((GROUP, span + LANES), jnp.float32),
            pltpu.VMEM((GROUP * STEP, span), jnp.bfloat16),
            pltpu.VMEM((LANES, PIECES * GROUP * STEP), jnp.bfloat16),
            pltpu.VMEM((length // LANES * GROUP, GROUP * STEP), jnp.float32),
            pltpu.VMEM((GROUP, block), jnp.float32),
        ],
        compiler_params=pltpu.CompilerParams(vmem_limit_bytes=VMEM_LIMIT),
    )(number.reshape(1), slot, codes, weight, waves, wide, scale)
    return scattered(partial_value)


def solution(mesh):
    in_specs = (
        P(("tmpl", "chan"), ("groups", "tm")),
        P(("tmpl", "chan"), "groups"),
        P("tmpl", "chan", None),
        P("tmpl", "chan"),
        P("tmpl", "chan"),
        P("tmpl"),
    )
    out_specs = P(("tmpl", "chan"), ("groups", "tm"))
    return jax.shard_map(body, mesh=mesh, in_specs=in_specs, out_specs=out_specs, check_vma=False)
```
